32 devices in a mesh: groups: 2 (over x), row: 16 (over z, y, core).
Axes of the slice: x: 2, y: 2, z: 4, core: 2. Of those that a mesh axis runs over, the one named last changes fastest.
Arguments:
- root_inverse: float32 [2048, 1024], P(('groups', 'row')), parts along dimension 0, as said below
- root_pivots: float32 [2048], P(('groups', 'row')), parts along dimension 0, may hold values from 0.25 to 4
- pattern: int32 [32, 8, 8], P(('groups', 'row')), parts along dimension 0, may hold values 0 or 1
- cross_factor: float32 [32, 1024, 1024], P('groups', 'row'), parts along dimension 0, may hold values from -0.375 to 0.375
- child_inverse: float32 [32, 512, 2, 1024], P('groups', 'row'), parts along dimension 0, as said below
- child_pivots: float32 [32, 1024], P('groups', 'row'), parts along dimension 0, may hold values from 0.25 to 4
Outputs:
- root_cov: float32 [2048, 1024], P(('groups', 'row')), parts along dimension 0
- cross_cov: float32 [32, 1024, 1024], P('groups', 'row'), parts along dimension 0
- variances: float32 [32, 1024], P(('groups', 'row')), parts along dimension 0
The draws below stay inside these ranges and needn't reach their ends.
There are 2 independent parts, one for each index of `groups`. The reference program is written for one: setup_inputs(seed, part) draws one part's arguments, and reference() takes and returns one part's arrays. A program takes and returns all parts, laid end to end along the dimension named above; each array names one. Nothing has to cross between parts.
Inputs may be any that keep to these rules, and one draw needn't show every extreme that they name: root_inverse is unit lower triangular. `child_inverse`: each G_c, once unfolded, is unit lower triangular.
All inputs are finite; a program needn't handle non-finite values. No bound on the sum of `pattern` on one device may be relied on, other than what follows from the above.
Results may differ from the reference program's by a relative error of at most 0.00009.
Values sent between devices are 32-bit elements; how exact they have to be, the bound alone decides.
No kernel may reach another device: no remote copies, remote signals or barrier semaphores. Data moves between devices by JAX's collectives and lax.ppermute only.
A program may use at most 128 MiB of HBM per device.

```python
import math
import jax
import jax.numpy as jnp
from jax import lax

WR = 1024
WC = 1024
BLK = 128
CH = 16


def draw_root_inverse(key, part):
    key = jax.random.fold_in(key, 11)
    noise = jax.random.normal(key, (WR, WR), jnp.float32)
    lower = jnp.tril(noise, -1) * (1.5 / WR ** 0.5)
    return lower + jnp.eye(WR, dtype=jnp.float32)


def draw_child_inverse(key, part):
    key = jax.random.fold_in(key, 23)
    noise = jax.random.normal(key, (CH, WC, WC), jnp.float32)
    lower = jnp.tril(noise, -1) * (1.5 / WC ** 0.5)
    whole = lower + jnp.eye(WC, dtype=jnp.float32)[None]
    upper_half = whole[:, :WC // 2, :]
    lower_half = whole[:, WC // 2:, :][:, ::-1, :]
    return jnp.stack([upper_half, lower_half], axis=2)


def place_ends(entries, rng, smallest, high):
    place = [jax.random.randint(jax.random.fold_in(rng, axis), (), 0, length) for axis, length in enumerate(entries.shape)]
    main_axis = entries.shape.index(max(entries.shape))
    next_to = place[:main_axis] + [(place[main_axis] + 1) % entries.shape[main_axis]] + place[main_axis + 1:]
    return entries.at[tuple(place)].set(smallest).at[tuple(next_to)].set(high)


def levels(stream_key, extent, cuts, low, largest):
    def one(axis_at, shards_of):
        draws = jax.random.uniform(jax.random.fold_in(jax.random.fold_in(stream_key, 6), axis_at), (shards_of,), jnp.float32, low / len(cuts), largest / len(cuts))
        return jnp.repeat(jnp.exp(draws), extent[axis_at] // shards_of).reshape((-1,) + (1,) * (len(extent) - axis_at - 1))

    loudness = one(*cuts[0])
    for cut in cuts[1:]:
        loudness = loudness * one(*cut)
    return loudness


def scatter_about(stream_key, dims, deviation, reach, split=(), held_as=jnp.bfloat16):
    level = levels(stream_key, dims, split, -0.22, 0.18) if split else 1.0
    drawn = jax.random.normal(stream_key, dims, jnp.float32) * deviation * level
    return jnp.minimum(jnp.maximum(drawn, -reach), reach).astype(held_as)


def setup_inputs(seed: int = 0, part: int = 0) -> dict:
    key_list = jax.random.split(jax.random.key(seed), 7)
    part_splits = jax.random.split(jax.random.fold_in(key_list[6], part), 7)
    root_inverse = draw_root_inverse(jax.random.fold_in(jax.random.fold_in(key_list[6], part), 71), part)
    root_pivots = jnp.clip(jnp.exp(math.log(4.0) - 2.7725887 * jax.random.uniform(part_splits[1], (WR,), jnp.float32) ** levels(part_splits[1], (WR,), ((0, 16),), -0.2, 0.2)), 0.25, 4.0)
    pattern = place_ends((jax.random.randint(part_splits[2], (CH, WR // BLK, WC // BLK), 0, 4) < 3).astype(jnp.int32), jax.random.fold_in(part_splits[2], 1), 0, 1)
    cross_factor = scatter_about(part_splits[3], (CH, WR, WC), (WR // 4) ** -0.5, 0.375, ((1, 16),), jnp.float32)
    child_inverse = draw_child_inverse(jax.random.fold_in(jax.random.fold_in(key_list[6], part), 71), part)
    child_pivots = jnp.clip(jnp.exp(math.log(4.0) - 2.7725887 * jax.random.uniform(part_splits[5], (CH, WC), jnp.float32) ** levels(part_splits[5], (CH, WC), ((1, 16),), -0.2, 0.2)), 0.25, 4.0)
    return {"root_inverse": root_inverse, "root_pivots": root_pivots, "pattern": pattern, "cross_factor": cross_factor, "child_inverse": child_inverse, "child_pivots": child_pivots}


def expand_mask(blocks):
    tall = jnp.broadcast_to(blocks[:, None, :, None], (WR // BLK, BLK, WC // BLK, BLK))
    return tall.reshape(WR, WC).astype(jnp.float32)


def unfold(folded):
    return jnp.concatenate([folded[:, 0, :], folded[::-1, 1, :]], axis=0)


def reference(root_inverse, root_pivots, pattern, cross_factor, child_inverse, child_pivots):
    hp = lax.Precision.HIGHEST
    root_cov = jnp.dot(root_inverse.T, root_inverse / root_pivots[:, None], preferred_element_type=jnp.float32, precision=hp)

    def one_child(items):
        blocks, panel, folded, pivots = items
        inverse = unfold(folded)
        masked = panel * expand_mask(blocks)
        scaled = jnp.dot(masked, inverse, preferred_element_type=jnp.float32, precision=hp)
        cross = -jnp.dot(root_cov, scaled, preferred_element_type=jnp.float32, precision=hp)
        own_part = jnp.sum(inverse * inverse / pivots[:, None], axis=0)
        variance = own_part - jnp.sum(scaled * cross, axis=0)
        return cross, variance

    cross_cov, variances = lax.map(one_child, (pattern, cross_factor, child_inverse, child_pivots))
    return root_cov, cross_cov, variances
```

```python
import jax
import jax.numpy as jnp
from jax import lax
from jax.experimental import pallas as pl
from jax.experimental.pallas import tpu as pltpu
from jax.sharding import PartitionSpec as P

BLK = 128
WIDE = 256
VMEM = 48 * 1024 * 1024


def split(x):
    high = x.astype(jnp.bfloat16)
    return high, (x - high.astype(jnp.float32)).astype(jnp.bfloat16)


def dot(a, b):
    return jnp.dot(a, b, preferred_element_type=jnp.float32)


def dot3(a_high, a_low, b_high, b_low):
    return dot(a_high, b_high) + (dot(a_high, b_low) + dot(a_low, b_high))


def k_range(block, half):
    start = block * WIDE
    if start < half:
        return start, 2 * half
    return half, half + 2 * half - start


def unfold(packed_ref, high_ref, low_ref):
    half, width = packed_ref.shape
    bands = half // BLK
    rows = lax.broadcasted_iota(jnp.int32, (BLK, BLK), 0)
    cols = lax.broadcasted_iota(jnp.int32, (BLK, BLK), 1)
    flip = (rows + cols == BLK - 1).astype(jnp.bfloat16)
    empty = jnp.zeros((BLK, BLK), jnp.bfloat16)
    for q in range(bands):
        here = pl.ds(q * BLK, BLK)
        there = pl.ds(half + q * BLK, BLK)
        last = 2 * bands - 1 - q
        full = packed_ref[here, : last * BLK]
        high_ref[there, : last * BLK], low_ref[there, : last * BLK] = split(full)
        mixed = packed_ref[here, last * BLK : (last + 1) * BLK]
        upper = jnp.where(
            rows + cols < BLK - 1, mixed, (rows + cols == BLK - 1).astype(jnp.float32)
        )
        edge = pl.ds(last * BLK, BLK)
        high_ref[there, edge], low_ref[there, edge] = split(upper)
        if last % 2 == 0:
            after = pl.ds((last + 1) * BLK, BLK)
            high_ref[there, after] = empty
            low_ref[there, after] = empty
        if q:
            rest = packed_ref[here, (last + 1) * BLK :]
            high_ref[here, : q * BLK], low_ref[here, : q * BLK] = split(rest)
        mixed_high, mixed_low = split(mixed)
        edge = pl.ds(q * BLK, BLK)
        diagonal = (rows == cols).astype(jnp.float32)
        high_ref[here, edge] = jnp.where(cols < rows, dot(mixed_high, flip), diagonal).astype(
            jnp.bfloat16
        )
        low_ref[here, edge] = jnp.where(cols < rows, dot(mixed_low, flip), 0.0).astype(
            jnp.bfloat16
        )
        if q % 2 == 0:
            after = pl.ds((q + 1) * BLK, BLK)
            high_ref[here, after] = empty
            low_ref[here, after] = empty


def cross_kernel(t_high_ref, t_low_ref, packed_ref, out_ref, g_high, g_low):
    half, width = packed_ref.shape

    @pl.when(pl.program_id(0) == 0)
    def _():
        unfold(packed_ref, g_high, g_low)

    for block in range(width // WIDE):
        first, stop = k_range(block, half)
        cols = pl.ds(block * WIDE, WIDE)
        out_ref[:, cols] = dot3(
            t_high_ref[:, first:stop],
            t_low_ref[:, first:stop],
            g_high[first:stop, cols],
            g_low[first:stop, cols],
        )


def variance_kernel(m_high_ref, m_low_ref, packed_ref, cross_ref, weight_ref, out_ref, g_high, g_low):
    half, width = packed_ref.shape

    @pl.when(pl.program_id(0) == 0)
    def _():
        unfold(packed_ref, g_high, g_low)
        for block in range(width // WIDE):
            first, stop = k_range(block, half)
            cols = pl.ds(block * WIDE, WIDE)
            entries = g_high[first:stop, cols].astype(jnp.float32) + g_low[
                first:stop, cols
            ].astype(jnp.float32)
            out_ref[:, cols] = jnp.sum(
                entries * entries * weight_ref[first:stop, :], axis=0, keepdims=True
            )

    for block in range(width // WIDE):
        first, stop = k_range(block, half)
        cols = pl.ds(block * WIDE, WIDE)
        scaled = dot3(
            m_high_ref[:, first:stop],
            m_low_ref[:, first:stop],
            g_high[first:stop, cols],
            g_low[first:stop, cols],
        )
        out_ref[:, cols] -= jnp.sum(scaled * cross_ref[:, cols], axis=0, keepdims=True)


def halves(x):
    high = lax.reduce_precision(x, 8, 7)
    return high.astype(jnp.bfloat16), (x - high).astype(jnp.bfloat16)


def pack(child_inverse, where):
    children, fold, _, width = child_inverse.shape
    blocks = width // BLK
    low = child_inverse[:, :, 0, :]
    high = child_inverse[:, :, 1, :]
    q = (where * fold) // BLK
    rows = (where * fold) % BLK + jnp.arange(fold)[:, None]
    spot = jnp.arange(BLK)[None, :]
    low_edge = lax.dynamic_slice_in_dim(low, q * BLK, BLK, 2)[:, :, ::-1]
    moved = lax.dynamic_slice_in_dim(
        jnp.concatenate([low, low], axis=2), q * BLK, width, 2
    )
    high_edge = lax.dynamic_slice_in_dim(high, (blocks - 1 - q) * BLK, BLK, 2)
    edge = jnp.where(spot + rows < BLK - 1, high_edge, low_edge)
    block = jnp.arange(width) // BLK
    packed = jnp.where(block < blocks - 1 - q, high, moved)
    return lax.dynamic_update_slice_in_dim(packed, edge, (blocks - 1 - q) * BLK, 2)


def on_device(root_inverse, root_pivots, pattern, cross_factor, child_inverse, child_pivots):
    count = lax.axis_size("row")
    where = lax.axis_index("row")
    own_rows, width_root = root_inverse.shape
    children, _, width_child = cross_factor.shape
    assert children == count
    half = width_child // 2
    plane = 4
    across = [list(range(k, count, plane)) for k in range(plane)]
    within = [list(range(k, k + plane)) for k in range(0, count, plane)]

    panels = lax.all_to_all(cross_factor, "row", split_axis=0, concat_axis=0, tiled=True)

    factor = root_inverse * lax.rsqrt(root_pivots)[:, None]
    factor = lax.all_gather(factor, "row", axis=0, tiled=True, axis_index_groups=across)
    factor = lax.all_gather(factor, "row", axis=0, tiled=True, axis_index_groups=within)
    pivots = lax.all_gather(child_pivots.reshape(8, -1), "row", axis=0, tiled=True)

    packed = pack(child_inverse, where)
    packed = lax.all_to_all(packed, "row", split_axis=0, concat_axis=0, tiled=True)
    packed = packed.reshape(half, width_child)

    whole_cov = jnp.dot(
        factor.T, factor, preferred_element_type=jnp.float32, precision=lax.Precision.HIGH
    )
    root_cov = lax.dynamic_slice_in_dim(whole_cov, where * own_rows, own_rows, 0)

    mask = jnp.repeat(jnp.repeat(pattern[0], BLK, 0), BLK, 1).astype(jnp.float32)
    masked = panels.reshape(width_root, width_child) * mask
    masked = jnp.concatenate([masked[:, :half], masked[:, half:][:, ::-1]], axis=1)
    turned = -jnp.dot(
        whole_cov, masked, preferred_element_type=jnp.float32, precision=lax.Precision.HIGH
    )
    t_high, t_low = halves(turned)
    m_high, m_low = halves(masked)

    steps = 4
    rows = width_root // steps
    row_spec = pl.BlockSpec((rows, width_child), lambda i: (i, 0))
    whole = lambda *shape: pl.BlockSpec(shape, lambda i: (0, 0))
    scratch = [pltpu.VMEM((width_child, width_child), jnp.bfloat16)] * 2
    flops = 4 * width_root * width_child * width_child
    cross = pl.pallas_call(
        cross_kernel,
        grid=(steps,),
        in_specs=[row_spec, row_spec, whole(half, width_child)],
        out_specs=row_spec,
        out_shape=jax.ShapeDtypeStruct((width_root, width_child), jnp.float32),
        scratch_shapes=scratch,
        compiler_params=pltpu.CompilerParams(vmem_limit_bytes=VMEM),
        cost_estimate=pl.CostEstimate(flops=flops, bytes_accessed=10 << 20, transcendentals=0),
        name="cross",
    )(t_high, t_low, packed)

    returned = lax.all_to_all(
        cross.reshape(children, own_rows, width_child),
        "row",
        split_axis=0,
        concat_axis=0,
        tiled=True,
    )

    mine = lax.dynamic_index_in_dim(pivots.reshape(count, children, own_rows), where, 1, False)
    weights = 1.0 / mine.reshape(width_child)
    weights = jnp.concatenate([weights[:half], weights[half:][::-1]])[:, None]
    variances = pl.pallas_call(
        variance_kernel,
        grid=(steps,),
        in_specs=[
            row_spec,
            row_spec,
            whole(half, width_child),
            row_spec,
            whole(width_child, 1),
        ],
        out_specs=whole(1, width_child),
        out_shape=jax.ShapeDtypeStruct((1, width_child), jnp.float32),
        scratch_shapes=scratch,
        compiler_params=pltpu.CompilerParams(vmem_limit_bytes=VMEM),
        cost_estimate=pl.CostEstimate(flops=flops, bytes_accessed=10 << 20, transcendentals=0),
        name="variance",
    )(m_high, m_low, packed, cross, weights)
    return root_cov, returned, variances


def solution(mesh):
    in_specs = (
        P(("groups", "row"), None),
        P(("groups", "row")),
        P(("groups", "row"), None, None),
        P("groups", "row", None),
        P("groups", "row", None, None),
        P("groups", "row"),
    )
    out_specs = (P(("groups", "row"), None), P("groups", "row", None), P(("groups", "row"), None))
    return jax.shard_map(
        on_device, mesh=mesh, in_specs=in_specs, out_specs=out_specs, check_vma=False
    )
```

```python
import jax
import jax.numpy as jnp
from jax import lax
from jax.experimental import pallas as pl
from jax.experimental.pallas import tpu as pltpu
from jax.sharding import PartitionSpec as P

BLK = 128
WIDE = 256
VMEM = 60 * 1024 * 1024


def split(x):
    high = x.astype(jnp.bfloat16)
    return high, (x - high.astype(jnp.float32)).astype(jnp.bfloat16)


def dot(a, b):
    return jnp.dot(a, b, preferred_element_type=jnp.float32)


def dot3(a_high, a_low, b_high, b_low):
    return dot(a_high, b_high) + (dot(a_high, b_low) + dot(a_low, b_high))


def k_range(block, half):
    start = block * WIDE
    if start < half:
        return start, 2 * half
    return half, half + 2 * half - start


def unfold(packed_ref, high_ref, low_ref):
    half, width = packed_ref.shape
    bands = half // BLK
    rows = lax.broadcasted_iota(jnp.int32, (BLK, BLK), 0)
    cols = lax.broadcasted_iota(jnp.int32, (BLK, BLK), 1)
    flip = (rows + cols == BLK - 1).astype(jnp.bfloat16)
    empty = jnp.zeros((BLK, BLK), jnp.bfloat16)
    for q in range(bands):
        here = pl.ds(q * BLK, BLK)
        there = pl.ds(half + q * BLK, BLK)
        last = 2 * bands - 1 - q
        full = packed_ref[here, : last * BLK]
        high_ref[there, : last * BLK], low_ref[there, : last * BLK] = split(full)
        mixed = packed_ref[here, last * BLK : (last + 1) * BLK]
        upper = jnp.where(
            rows + cols < BLK - 1, mixed, (rows + cols == BLK - 1).astype(jnp.float32)
        )
        edge = pl.ds(last * BLK, BLK)
        high_ref[there, edge], low_ref[there, edge] = split(upper)
        if last % 2 == 0:
            after = pl.ds((last + 1) * BLK, BLK)
            high_ref[there, after] = empty
            low_ref[there, after] = empty
        if q:
            rest = packed_ref[here, (last + 1) * BLK :]
            high_ref[here, : q * BLK], low_ref[here, : q * BLK] = split(rest)
        mixed_high, mixed_low = split(mixed)
        edge = pl.ds(q * BLK, BLK)
        diagonal = (rows == cols).astype(jnp.float32)
        high_ref[here, edge] = jnp.where(cols < rows, dot(mixed_high, flip), diagonal).astype(
            jnp.bfloat16
        )
        low_ref[here, edge] = jnp.where(cols < rows, dot(mixed_low, flip), 0.0).astype(
            jnp.bfloat16
        )
        if q % 2 == 0:
            after = pl.ds((q + 1) * BLK, BLK)
            high_ref[here, after] = empty
            low_ref[here, after] = empty


def cross_kernel(t_high_ref, t_low_ref, packed_ref, out_ref, g_high, g_low):
    half, width = packed_ref.shape

    @pl.when(pl.program_id(0) == 0)
    def _():
        unfold(packed_ref, g_high, g_low)

    for block in range(width // WIDE):
        first, stop = k_range(block, half)
        cols = pl.ds(block * WIDE, WIDE)
        out_ref[:, cols] = dot3(
            t_high_ref[:, first:stop],
            t_low_ref[:, first:stop],
            g_high[first:stop, cols],
            g_low[first:stop, cols],
        )


def variance_kernel(m_high_ref, m_low_ref, packed_ref, cross_ref, weight_ref, out_ref, g_high, g_low):
    half, width = packed_ref.shape

    @pl.when(pl.program_id(0) == 0)
    def _():
        unfold(packed_ref, g_high, g_low)
        for block in range(width // WIDE):
            first, stop = k_range(block, half)
            cols = pl.ds(block * WIDE, WIDE)
            entries = g_high[first:stop, cols].astype(jnp.float32) + g_low[
                first:stop, cols
            ].astype(jnp.float32)
            out_ref[:, cols] = jnp.sum(
                entries * entries * weight_ref[first:stop, :], axis=0, keepdims=True
            )

    for block in range(width // WIDE):
        first, stop = k_range(block, half)
        cols = pl.ds(block * WIDE, WIDE)
        scaled = dot3(
            m_high_ref[:, first:stop],
            m_low_ref[:, first:stop],
            g_high[first:stop, cols],
            g_low[first:stop, cols],
        )
        out_ref[:, cols] -= jnp.sum(scaled * cross_ref[:, cols], axis=0, keepdims=True)


def halves(x):
    high = lax.reduce_precision(x, 8, 7)
    return high.astype(jnp.bfloat16), (x - high).astype(jnp.bfloat16)


def pack(child_inverse, where):
    children, fold, _, width = child_inverse.shape
    blocks = width // BLK
    low = child_inverse[:, :, 0, :]
    high = child_inverse[:, :, 1, :]
    q = (where * fold) // BLK
    rows = (where * fold) % BLK + jnp.arange(fold)[:, None]
    spot = jnp.arange(BLK)[None, :]
    low_edge = lax.dynamic_slice_in_dim(low, q * BLK, BLK, 2)[:, :, ::-1]
    moved = lax.dynamic_slice_in_dim(
        jnp.concatenate([low, low], axis=2), q * BLK, width, 2
    )
    high_edge = lax.dynamic_slice_in_dim(high, (blocks - 1 - q) * BLK, BLK, 2)
    edge = jnp.where(spot + rows < BLK - 1, high_edge, low_edge)
    block = jnp.arange(width) // BLK
    packed = jnp.where(block < blocks - 1 - q, high, moved)
    return lax.dynamic_update_slice_in_dim(packed, edge, (blocks - 1 - q) * BLK, 2)


def on_device(root_inverse, root_pivots, pattern, cross_factor, child_inverse, child_pivots):
    count = lax.axis_size("row")
    where = lax.axis_index("row")
    own_rows, width_root = root_inverse.shape
    children, _, width_child = cross_factor.shape
    assert children == count
    half = width_child // 2
    plane = 4
    across = [list(range(k, count, plane)) for k in range(plane)]
    within = [list(range(k, k + plane)) for k in range(0, count, plane)]

    panels = lax.all_to_all(cross_factor, "row", split_axis=0, concat_axis=0, tiled=True)

    factor = root_inverse * lax.rsqrt(root_pivots)[:, None]
    pivot_rows = child_pivots.reshape(-1, width_root)
    pivot_rows = jnp.pad(pivot_rows, ((0, -pivot_rows.shape[0] % 8), (0, 0)))
    sent = jnp.concatenate([factor, pivot_rows])
    sent = lax.all_gather(sent, "row", axis=0, tiled=True, axis_index_groups=across)
    sent = lax.all_gather(sent, "row", axis=0, tiled=True, axis_index_groups=within)
    sent = sent.reshape(plane, count // plane, -1, width_root)
    factor = sent[:, :, :own_rows].reshape(width_root, width_root)
    pivots = jnp.swapaxes(sent[:, :, own_rows:], 0, 1).reshape(count, -1)
    pivots = pivots[:, : children * own_rows].reshape(count, children, own_rows)

    packed = pack(child_inverse, where)
    packed = lax.all_to_all(packed, "row", split_axis=0, concat_axis=0, tiled=True)
    packed = packed.reshape(half, width_child)

    whole_cov = jnp.dot(
        factor.T, factor, preferred_element_type=jnp.float32, precision=lax.Precision.HIGH
    )
    root_cov = lax.dynamic_slice_in_dim(whole_cov, where * own_rows, own_rows, 0)

    mask = jnp.repeat(jnp.repeat(pattern[0], BLK, 0), BLK, 1).astype(jnp.float32)
    masked = panels.reshape(width_root, width_child) * mask
    masked = jnp.concatenate([masked[:, :half], masked[:, half:][:, ::-1]], axis=1)
    turned = -jnp.dot(
        whole_cov, masked, preferred_element_type=jnp.float32, precision=lax.Precision.HIGH
    )
    t_high, t_low = halves(turned)
    m_high, m_low = halves(masked)

    steps = 4
    rows = width_root // steps
    row_spec = pl.BlockSpec((rows, width_child), lambda i: (i, 0))
    whole = lambda *shape: pl.BlockSpec(shape, lambda i: (0, 0))
    scratch = [pltpu.VMEM((width_child, width_child), jnp.bfloat16)] * 2
    flops = 4 * width_root * width_child * width_child
    cross = pl.pallas_call(
        cross_kernel,
        grid=(steps,),
        in_specs=[row_spec, row_spec, whole(half, width_child)],
        out_specs=row_spec,
        out_shape=jax.ShapeDtypeStruct((width_root, width_child), jnp.float32),
        scratch_shapes=scratch,
        compiler_params=pltpu.CompilerParams(vmem_limit_bytes=VMEM),
        cost_estimate=pl.CostEstimate(flops=flops, bytes_accessed=10 << 20, transcendentals=0),
        name="cross",
    )(t_high, t_low, packed)

    returned = lax.all_to_all(
        cross.reshape(children, own_rows, width_child),
        "row",
        split_axis=0,
        concat_axis=0,
        tiled=True,
    )

    mine = lax.dynamic_index_in_dim(pivots, where, 1, False)
    weights = 1.0 / mine.reshape(width_child)
    weights = jnp.concatenate([weights[:half], weights[half:][::-1]])[:, None]
    variances = pl.pallas_call(
        variance_kernel,
        grid=(steps,),
        in_specs=[
            row_spec,
            row_spec,
            whole(half, width_child),
            row_spec,
            whole(width_child, 1),
        ],
        out_specs=whole(1, width_child),
        out_shape=jax.ShapeDtypeStruct((1, width_child), jnp.float32),
        scratch_shapes=scratch,
        compiler_params=pltpu.CompilerParams(vmem_limit_bytes=VMEM),
        cost_estimate=pl.CostEstimate(flops=flops, bytes_accessed=10 << 20, transcendentals=0),
        name="variance",
    )(m_high, m_low, packed, cross, weights)
    return root_cov, returned, variances


def solution(mesh):
    in_specs = (
        P(("groups", "row"), None),
        P(("groups", "row")),
        P(("groups", "row"), None, None),
        P("groups", "row", None),
        P("groups", "row", None, None),
        P("groups", "row"),
    )
    out_specs = (P(("groups", "row"), None), P("groups", "row", None), P(("groups", "row"), None))
    return jax.shard_map(
        on_device, mesh=mesh, in_specs=in_specs, out_specs=out_specs, check_vma=False
    )
```

```python
import jax
import jax.numpy as jnp
from jax import lax
from jax.experimental import pallas as pl
from jax.experimental.pallas import tpu as pltpu
from jax.sharding import PartitionSpec as P

BLK = 128
WIDE = 256
VMEM = 60 * 1024 * 1024
LIGHT = pl.CostEstimate(flops=1, bytes_accessed=1, transcendentals=0)


def split(x):
    high = x.astype(jnp.bfloat16)
    return high, (x - high.astype(jnp.float32)).astype(jnp.bfloat16)


def dot(a, b):
    return jnp.dot(a, b, preferred_element_type=jnp.float32)


def dot3(a_high, a_low, b_high, b_low):
    return dot(a_high, b_high) + (dot(a_high, b_low) + dot(a_low, b_high))


def k_range(block, half):
    start = block * WIDE
    if start < half:
        return start, 2 * half
    return half, half + 2 * half - start


def unfold(packed_ref, high_ref, low_ref):
    half, width = packed_ref.shape
    bands = half // BLK
    rows = lax.broadcasted_iota(jnp.int32, (BLK, BLK), 0)
    cols = lax.broadcasted_iota(jnp.int32, (BLK, BLK), 1)
    flip = (rows + cols == BLK - 1).astype(jnp.bfloat16)
    empty = jnp.zeros((BLK, BLK), jnp.bfloat16)
    for q in range(bands):
        here = pl.ds(q * BLK, BLK)
        there = pl.ds(half + q * BLK, BLK)
        last = 2 * bands - 1 - q
        full = packed_ref[here, : last * BLK]
        high_ref[there, : last * BLK], low_ref[there, : last * BLK] = split(full)
        mixed = packed_ref[here, last * BLK : (last + 1) * BLK]
        upper = jnp.where(
            rows + cols < BLK - 1, mixed, (rows + cols == BLK - 1).astype(jnp.float32)
        )
        edge = pl.ds(last * BLK, BLK)
        high_ref[there, edge], low_ref[there, edge] = split(upper)
        if last % 2 == 0:
            after = pl.ds((last + 1) * BLK, BLK)
            high_ref[there, after] = empty
            low_ref[there, after] = empty
        if q:
            rest = packed_ref[here, (last + 1) * BLK :]
            high_ref[here, : q * BLK], low_ref[here, : q * BLK] = split(rest)
        mixed_high, mixed_low = split(mixed)
        edge = pl.ds(q * BLK, BLK)
        diagonal = (rows == cols).astype(jnp.float32)
        high_ref[here, edge] = jnp.where(cols < rows, dot(mixed_high, flip), diagonal).astype(
            jnp.bfloat16
        )
        low_ref[here, edge] = jnp.where(cols < rows, dot(mixed_low, flip), 0.0).astype(
            jnp.bfloat16
        )
        if q % 2 == 0:
            after = pl.ds((q + 1) * BLK, BLK)
            high_ref[here, after] = empty
            low_ref[here, after] = empty


def mask_kernel(pattern_ref, panel_ref, high_ref, low_ref):
    height, width = panel_ref.shape
    blocks = width // BLK
    rows = lax.broadcasted_iota(jnp.int32, (BLK, BLK), 0)
    cols = lax.broadcasted_iota(jnp.int32, (BLK, BLK), 1)
    flip = (rows + cols == BLK - 1).astype(jnp.bfloat16)
    for b in range(blocks):
        block = panel_ref[:, b * BLK : (b + 1) * BLK]
        here = pattern_ref[pl.program_id(0), b].astype(jnp.float32)
        high, low = split(block * here)
        place = b
        if b >= blocks // 2:
            high = dot(high, flip).astype(jnp.bfloat16)
            low = dot(low, flip).astype(jnp.bfloat16)
            place = blocks // 2 + blocks - 1 - b
        to = pl.ds(place * BLK, BLK)
        high_ref[:, to] = high
        low_ref[:, to] = low


def turn_kernel(cov_ref, m_high_ref, m_low_ref, t_high_ref, t_low_ref):
    cov_high, cov_low = split(cov_ref[...])
    for block in range(m_high_ref.shape[1] // WIDE):
        cols = pl.ds(block * WIDE, WIDE)
        t_high_ref[:, cols], t_low_ref[:, cols] = split(
            -dot3(cov_high, cov_low, m_high_ref[:, cols], m_low_ref[:, cols])
        )


def cross_kernel(t_high_ref, t_low_ref, packed_ref, out_ref, g_high, g_low):
    half, width = packed_ref.shape

    @pl.when(pl.program_id(0) == 0)
    def _():
        unfold(packed_ref, g_high, g_low)

    for block in range(width // WIDE):
        first, stop = k_range(block, half)
        cols = pl.ds(block * WIDE, WIDE)
        out_ref[:, cols] = dot3(
            t_high_ref[:, first:stop],
            t_low_ref[:, first:stop],
            g_high[first:stop, cols],
            g_low[first:stop, cols],
        )


def variance_kernel(m_high_ref, m_low_ref, packed_ref, cross_ref, weight_ref, out_ref, g_high, g_low):
    half, width = packed_ref.shape

    @pl.when(pl.program_id(0) == 0)
    def _():
        unfold(packed_ref, g_high, g_low)
        for block in range(width // WIDE):
            first, stop = k_range(block, half)
            cols = pl.ds(block * WIDE, WIDE)
            entries = g_high[first:stop, cols].astype(jnp.float32) + g_low[
                first:stop, cols
            ].astype(jnp.float32)
            out_ref[:, cols] = jnp.sum(
                entries * entries * weight_ref[first:stop, :], axis=0, keepdims=True
            )

    for block in range(width // WIDE):
        first, stop = k_range(block, half)
        cols = pl.ds(block * WIDE, WIDE)
        scaled = dot3(
            m_high_ref[:, first:stop],
            m_low_ref[:, first:stop],
            g_high[first:stop, cols],
            g_low[first:stop, cols],
        )
        out_ref[:, cols] -= jnp.sum(scaled * cross_ref[:, cols], axis=0, keepdims=True)


def pack(child_inverse, where):
    children, fold, _, width = child_inverse.shape
    blocks = width // BLK
    low = child_inverse[:, :, 0, :]
    high = child_inverse[:, :, 1, :]
    q = (where * fold) // BLK
    rows = (where * fold) % BLK + jnp.arange(fold)[:, None]
    spot = jnp.arange(BLK)[None, :]
    low_edge = lax.dynamic_slice_in_dim(low, q * BLK, BLK, 2)[:, :, ::-1]
    moved = lax.dynamic_slice_in_dim(
        jnp.concatenate([low, low], axis=2), q * BLK, width, 2
    )
    high_edge = lax.dynamic_slice_in_dim(high, (blocks - 1 - q) * BLK, BLK, 2)
    edge = jnp.where(spot + rows < BLK - 1, high_edge, low_edge)
    block = jnp.arange(width) // BLK
    packed = jnp.where(block < blocks - 1 - q, high, moved)
    return lax.dynamic_update_slice_in_dim(packed, edge, (blocks - 1 - q) * BLK, 2)


def swap(x, count, bit):
    return lax.ppermute(x, "row", [(i, i ^ bit) for i in range(count)])


def spread(held, sources, count, bit):
    held = jnp.concatenate([held, swap(held, count, bit)])
    return held, sources + [s ^ bit for s in sources]


def exchange(x):
    return lax.all_to_all(x, "row", split_axis=0, concat_axis=0, tiled=True)


def on_device(root_inverse, root_pivots, pattern, cross_factor, child_inverse, child_pivots):
    count = lax.axis_size("row")
    where = lax.axis_index("row")
    own_rows, width_root = root_inverse.shape
    children, _, width_child = cross_factor.shape
    assert children == count
    half = width_child // 2

    factor = root_inverse * lax.rsqrt(root_pivots)[:, None]
    pivot_rows = child_pivots.reshape(-1, width_root)
    pivot_rows = jnp.pad(pivot_rows, ((0, -pivot_rows.shape[0] % 8), (0, 0)))
    packed = pack(child_inverse, where)

    bits = [count // 2, *(1 << k for k in range(1, count.bit_length() - 2)), 1]
    sent, sources = spread(jnp.concatenate([factor, pivot_rows]), [0], count, bits[0])
    sent, panels = lax.optimization_barrier((sent, cross_factor))
    panels = exchange(panels)
    for bit in bits[1:-1]:
        sent, sources = spread(sent, sources, count, bit)
    sent, sources = spread(sent, sources, count, bits[-1])
    packed = exchange(packed).reshape(half, width_child)

    sent = sent.reshape(count, -1, width_root)
    factor = sent[:, :own_rows].reshape(width_root, width_root)
    pivots = sent[:, own_rows:].reshape(count, -1)
    pivots = pivots[:, : children * own_rows].reshape(count, children, own_rows)

    whole_cov = jnp.dot(
        factor.T, factor, preferred_element_type=jnp.float32, precision=lax.Precision.HIGH
    )
    root_cov = lax.dynamic_slice_in_dim(whole_cov, where * own_rows, own_rows, 0)

    steps = 4
    rows = width_root // steps
    row_spec = pl.BlockSpec((rows, width_child), lambda i: (i, 0))
    whole = lambda *shape: pl.BlockSpec(shape, lambda i: (0, 0))
    scratch = [pltpu.VMEM((width_child, width_child), jnp.bfloat16)] * 2
    flops = 4 * width_root * width_child * width_child
    halved = jax.ShapeDtypeStruct((width_root, width_child), jnp.bfloat16)
    band = pl.BlockSpec((BLK, width_child), lambda i: (i, 0))
    m_high, m_low = pl.pallas_call(
        mask_kernel,
        grid=(width_root // BLK,),
        in_specs=[pl.BlockSpec(memory_space=pltpu.SMEM), band],
        out_specs=[band, band],
        out_shape=[halved] * 2,
        compiler_params=pltpu.CompilerParams(vmem_limit_bytes=VMEM),
        cost_estimate=LIGHT,
        name="mask",
    )(pattern[0], panels.reshape(width_root, width_child))
    t_high, t_low = pl.pallas_call(
        turn_kernel,
        grid=(steps,),
        in_specs=[
            pl.BlockSpec((rows, width_root), lambda i: (i, 0)),
            whole(width_root, width_child),
            whole(width_root, width_child),
        ],
        out_specs=[row_spec, row_spec],
        out_shape=[halved] * 2,
        compiler_params=pltpu.CompilerParams(vmem_limit_bytes=VMEM),
        cost_estimate=LIGHT,
        name="turn",
    )(whole_cov, m_high, m_low)
    cross = pl.pallas_call(
        cross_kernel,
        grid=(steps,),
        in_specs=[row_spec, row_spec, whole(half, width_child)],
        out_specs=row_spec,
        out_shape=jax.ShapeDtypeStruct((width_root, width_child), jnp.float32),
        scratch_shapes=scratch,
        compiler_params=pltpu.CompilerParams(vmem_limit_bytes=VMEM),
        cost_estimate=pl.CostEstimate(flops=flops, bytes_accessed=10 << 20, transcendentals=0),
        name="cross",
    )(t_high, t_low, packed)

    returned = exchange(cross.reshape(children, own_rows, width_child))

    mine = lax.dynamic_index_in_dim(pivots, where, 1, False)
    owner = jnp.bitwise_xor(where, jnp.array(sources))
    chosen = (owner[None, :] == jnp.arange(count)[:, None])[:, :, None]
    mine = jnp.sum(jnp.where(chosen, mine[None], 0.0), axis=1)
    weights = 1.0 / mine.reshape(width_child)
    weights = jnp.concatenate([weights[:half], weights[half:][::-1]])[:, None]
    variances = pl.pallas_call(
        variance_kernel,
        grid=(steps,),
        in_specs=[
            row_spec,
            row_spec,
            whole(half, width_child),
            row_spec,
            whole(width_child, 1),
        ],
        out_specs=whole(1, width_child),
        out_shape=jax.ShapeDtypeStruct((1, width_child), jnp.float32),
        scratch_shapes=scratch,
        compiler_params=pltpu.CompilerParams(vmem_limit_bytes=VMEM),
        cost_estimate=pl.CostEstimate(flops=flops, bytes_accessed=10 << 20, transcendentals=0),
        name="variance",
    )(m_high, m_low, packed, cross, weights)
    return root_cov, returned, variances


def solution(mesh):
    in_specs = (
        P(("groups", "row"), None),
        P(("groups", "row")),
        P(("groups", "row"), None, None),
        P("groups", "row", None),
        P("groups", "row", None, None),
        P("groups", "row"),
    )
    out_specs = (P(("groups", "row"), None), P("groups", "row", None), P(("groups", "row"), None))
    return jax.shard_map(
        on_device, mesh=mesh, in_specs=in_specs, out_specs=out_specs, check_vma=False
    )
```

```python
import jax
import jax.numpy as jnp
from jax import lax
from jax.experimental import pallas as pl
from jax.experimental.pallas import tpu as pltpu
from jax.sharding import PartitionSpec as P

BLK = 128
WIDE = 256
VMEM = 121 * 512 * 1024
VMEM_CROSS = 48 * 1024 * 1024
STEPS = 4
LIGHT = pl.CostEstimate(flops=1, bytes_accessed=1, transcendentals=0)


def split(x):
    high = x.astype(jnp.bfloat16)
    return high, (x - high.astype(jnp.float32)).astype(jnp.bfloat16)


def dot(a, b):
    return jnp.dot(a, b, preferred_element_type=jnp.float32)


def dot3(a_high, a_low, b_high, b_low):
    return dot(a_high, b_high) + (dot(a_high, b_low) + dot(a_low, b_high))


def k_range(block, half):
    start = block * WIDE
    if start < half:
        return start, 2 * half
    return half, half + 2 * half - start


def unfold(packed_ref, high_ref, low_ref):
    half, width = packed_ref.shape
    bands = half // BLK
    rows = lax.broadcasted_iota(jnp.int32, (BLK, BLK), 0)
    cols = lax.broadcasted_iota(jnp.int32, (BLK, BLK), 1)
    flip = (rows + cols == BLK - 1).astype(jnp.bfloat16)
    empty = jnp.zeros((BLK, BLK), jnp.bfloat16)
    for q in range(bands):
        here = pl.ds(q * BLK, BLK)
        there = pl.ds(half + q * BLK, BLK)
        last = 2 * bands - 1 - q
        full = packed_ref[here, : last * BLK]
        high_ref[there, : last * BLK], low_ref[there, : last * BLK] = split(full)
        mixed = packed_ref[here, last * BLK : (last + 1) * BLK]
        upper = jnp.where(
            rows + cols < BLK - 1, mixed, (rows + cols == BLK - 1).astype(jnp.float32)
        )
        edge = pl.ds(last * BLK, BLK)
        high_ref[there, edge], low_ref[there, edge] = split(upper)
        if last % 2 == 0:
            after = pl.ds((last + 1) * BLK, BLK)
            high_ref[there, after] = empty
            low_ref[there, after] = empty
        if q:
            rest = packed_ref[here, (last + 1) * BLK :]
            high_ref[here, : q * BLK], low_ref[here, : q * BLK] = split(rest)
        mixed_high, mixed_low = split(mixed)
        edge = pl.ds(q * BLK, BLK)
        diagonal = (rows == cols).astype(jnp.float32)
        high_ref[here, edge] = jnp.where(cols < rows, dot(mixed_high, flip), diagonal).astype(
            jnp.bfloat16
        )
        low_ref[here, edge] = jnp.where(cols < rows, dot(mixed_low, flip), 0.0).astype(
            jnp.bfloat16
        )
        if q % 2 == 0:
            after = pl.ds((q + 1) * BLK, BLK)
            high_ref[here, after] = empty
            low_ref[here, after] = empty


def mask_kernel(pattern_ref, panel_ref, m_ref):
    height, width = panel_ref.shape
    blocks = width // BLK
    rows = lax.broadcasted_iota(jnp.int32, (BLK, BLK), 0)
    cols = lax.broadcasted_iota(jnp.int32, (BLK, BLK), 1)
    flip = (rows + cols == BLK - 1).astype(jnp.bfloat16)
    for b in range(blocks):
        block = panel_ref[:, b * BLK : (b + 1) * BLK]
        here = pattern_ref[pl.program_id(0), b].astype(jnp.float32)
        high, low = split(block * here)
        place = b
        if b >= blocks // 2:
            high = dot(high, flip).astype(jnp.bfloat16)
            low = dot(low, flip).astype(jnp.bfloat16)
            place = blocks // 2 + blocks - 1 - b
        to = pl.ds(place * BLK, BLK)
        m_ref[0, :, to] = high
        m_ref[1, :, to] = low


def turn_kernel(cov_ref, m_ref, t_ref):
    cov_high, cov_low = split(cov_ref[...])
    for block in range(m_ref.shape[2] // WIDE):
        cols = pl.ds(block * WIDE, WIDE)
        t_ref[0, :, cols], t_ref[1, :, cols] = split(
            -dot3(cov_high, cov_low, m_ref[0, :, cols], m_ref[1, :, cols])
        )


def cross_kernel(t_ref, packed_ref, out_ref, g_ref, t, g, out, came, left, kept):
    half, width = packed_ref.shape
    rows = out.shape[0] // STEPS
    arriving, leaving = [], []
    for step in range(STEPS):
        here = pl.ds(step * rows, rows)
        arriving.append(pltpu.make_async_copy(t_ref.at[:, here], t.at[:, here], came.at[step]))
        leaving.append(pltpu.make_async_copy(out.at[here], out_ref.at[here], left.at[step]))
    keeping = pltpu.make_async_copy(g, g_ref, kept)
    for copy in arriving:
        copy.start()
    unfold(packed_ref, g.at[0], g.at[1])
    keeping.start()
    for step in range(STEPS):
        here = pl.ds(step * rows, rows)
        arriving[step].wait()
        for block in range(width // WIDE):
            first, stop = k_range(block, half)
            cols = pl.ds(block * WIDE, WIDE)
            out[here, cols] = dot3(
                t[0, here, first:stop],
                t[1, here, first:stop],
                g[0, first:stop, cols],
                g[1, first:stop, cols],
            )
        leaving[step].start()
    for copy in leaving:
        copy.wait()
    keeping.wait()


def copy_kernel(from_ref, to_ref, held, came, left):
    parts = came.shape[0]
    each = held.shape[0] // parts
    pieces = [pl.ds(part * each, each) for part in range(parts)]
    arriving = [
        pltpu.make_async_copy(from_ref.at[here], held.at[here], came.at[part])
        for part, here in enumerate(pieces)
    ]
    leaving = [
        pltpu.make_async_copy(held.at[here], to_ref.at[here], left.at[part])
        for part, here in enumerate(pieces)
    ]
    for copy in arriving:
        copy.start()
    for came_in, leave in zip(arriving, leaving):
        came_in.wait()
        leave.start()
    for copy in leaving:
        copy.wait()


def variance_kernel(m_ref, g_ref, cross_ref, weight_ref, out_ref):
    _, height, width = g_ref.shape

    @pl.when(pl.program_id(0) == 0)
    def _():
        for block in range(width // WIDE):
            first, stop = k_range(block, height // 2)
            cols = pl.ds(block * WIDE, WIDE)
            entries = g_ref[0, first:stop, cols].astype(jnp.float32)
            entries += g_ref[1, first:stop, cols].astype(jnp.float32)
            out_ref[:, cols] = jnp.sum(
                entries * entries * weight_ref[first:stop, :], axis=0, keepdims=True
            )

    for block in range(width // WIDE):
        first, stop = k_range(block, height // 2)
        cols = pl.ds(block * WIDE, WIDE)
        scaled = dot3(
            m_ref[0, :, first:stop],
            m_ref[1, :, first:stop],
            g_ref[0, first:stop, cols],
            g_ref[1, first:stop, cols],
        )
        out_ref[:, cols] -= jnp.sum(scaled * cross_ref[:, cols], axis=0, keepdims=True)


def pack(child_inverse, where):
    children, fold, _, width = child_inverse.shape
    blocks = width // BLK
    low = child_inverse[:, :, 0, :]
    high = child_inverse[:, :, 1, :]
    q = (where * fold) // BLK
    rows = (where * fold) % BLK + jnp.arange(fold)[:, None]
    spot = jnp.arange(BLK)[None, :]
    low_edge = lax.dynamic_slice_in_dim(low, q * BLK, BLK, 2)[:, :, ::-1]
    moved = lax.dynamic_slice_in_dim(
        jnp.concatenate([low, low], axis=2), q * BLK, width, 2
    )
    high_edge = lax.dynamic_slice_in_dim(high, (blocks - 1 - q) * BLK, BLK, 2)
    edge = jnp.where(spot + rows < BLK - 1, high_edge, low_edge)
    block = jnp.arange(width) // BLK
    packed = jnp.where(block < blocks - 1 - q, high, moved)
    return lax.dynamic_update_slice_in_dim(packed, edge, (blocks - 1 - q) * BLK, 2)


def swap(x, count, bit):
    return lax.ppermute(x, "row", [(i, i ^ bit) for i in range(count)])


def scale(inverse, pivots):
    rows, width = inverse.shape
    child_pivots = pivots[0, :-rows].reshape(-1, width)
    child_pivots = jnp.pad(child_pivots, ((0, -child_pivots.shape[0] % 8), (0, 0)))
    return inverse * lax.rsqrt(pivots[0, -rows:])[:, None], child_pivots


def spread(held, sources, count, bit):
    held = jnp.concatenate([held, swap(held, count, bit)])
    return held, sources + [s ^ bit for s in sources]


def exchange(x):
    return lax.all_to_all(x, "row", split_axis=0, concat_axis=0, tiled=True)


def on_device(root_inverse, root_pivots, pattern, cross_factor, child_inverse, child_pivots):
    count = lax.axis_size("row")
    where = lax.axis_index("row")
    own_rows, width_root = root_inverse.shape
    children, _, width_child = cross_factor.shape
    assert children == count
    half = width_child // 2

    packed = pack(child_inverse, where)

    bits = [count // 2, *(1 << k for k in range(1, count.bit_length() - 2)), 1]
    pivots = jnp.concatenate([child_pivots.reshape(-1), root_pivots])[None]
    far_inverse, far_pivots, panels = lax.optimization_barrier(
        (swap(root_inverse, count, bits[0]), swap(pivots, count, bits[0]), cross_factor)
    )
    sent = [*scale(root_inverse, pivots), *scale(far_inverse, far_pivots)]
    sent, sources = jnp.concatenate(sent), [0, bits[0]]
    panels = exchange(panels)
    for bit in bits[1:]:
        sent, sources = spread(sent, sources, count, bit)
    packed = exchange(packed).reshape(half, width_child)

    sent = sent.reshape(count, -1, width_root)
    factor = sent[:, :own_rows].reshape(width_root, width_root)
    pivots = sent[:, own_rows:].reshape(count, -1)
    pivots = pivots[:, : children * own_rows].reshape(count, children, own_rows)

    whole_cov = jnp.dot(
        factor.T, factor, preferred_element_type=jnp.float32, precision=lax.Precision.HIGH
    )
    root_cov = lax.dynamic_slice_in_dim(whole_cov, where * own_rows, own_rows, 0)

    rows = width_root // STEPS
    row_spec = pl.BlockSpec((rows, width_child), lambda i: (i, 0))
    pair_spec = pl.BlockSpec((2, rows, width_child), lambda i: (0, i, 0))
    band = pl.BlockSpec((BLK, width_child), lambda i: (i, 0))
    pair = jax.ShapeDtypeStruct((2, width_root, width_child), jnp.bfloat16)
    pair_whole = pl.BlockSpec((2, width_root, width_child), lambda i: (0, 0, 0))
    anywhere = pl.BlockSpec(memory_space=pltpu.HBM)
    params = pltpu.CompilerParams(vmem_limit_bytes=VMEM)
    m = pl.pallas_call(
        mask_kernel,
        grid=(width_root // BLK,),
        in_specs=[pl.BlockSpec(memory_space=pltpu.SMEM), band],
        out_specs=pl.BlockSpec((2, BLK, width_child), lambda i: (0, i, 0)),
        out_shape=pair,
        compiler_params=params,
        cost_estimate=LIGHT,
        name="mask",
    )(pattern[0], panels.reshape(width_root, width_child))
    t = pl.pallas_call(
        turn_kernel,
        grid=(STEPS,),
        in_specs=[pl.BlockSpec((rows, width_root), lambda i: (i, 0)), pair_whole],
        out_specs=pair_spec,
        out_shape=pair,
        compiler_params=params,
        cost_estimate=LIGHT,
        name="turn",
    )(whole_cov, m)
    cross, g = pl.pallas_call(
        cross_kernel,
        in_specs=[anywhere, pl.BlockSpec(memory_space=pltpu.VMEM)],
        out_specs=[anywhere, anywhere],
        out_shape=[
            jax.ShapeDtypeStruct((width_root, width_child), jnp.float32),
            jax.ShapeDtypeStruct((2, width_child, width_child), jnp.bfloat16),
        ],
        scratch_shapes=[
            pltpu.VMEM((2, width_root, width_child), jnp.bfloat16),
            pltpu.VMEM((2, width_child, width_child), jnp.bfloat16),
            pltpu.VMEM((width_root, width_child), jnp.float32),
            pltpu.SemaphoreType.DMA((STEPS,)),
            pltpu.SemaphoreType.DMA((STEPS,)),
            pltpu.SemaphoreType.DMA(()),
        ],
        compiler_params=pltpu.CompilerParams(vmem_limit_bytes=VMEM_CROSS),
        name="cross",
    )(t, packed)

    returned = exchange(cross.reshape(children, own_rows, width_child))
    returned = pl.pallas_call(
        copy_kernel,
        in_specs=[anywhere],
        out_specs=anywhere,
        out_shape=jax.ShapeDtypeStruct(returned.shape, returned.dtype),
        scratch_shapes=[
            pltpu.VMEM(returned.shape, returned.dtype),
            pltpu.SemaphoreType.DMA((8,)),
            pltpu.SemaphoreType.DMA((8,)),
        ],
        compiler_params=params,
        name="place",
    )(returned)

    mine = lax.dynamic_index_in_dim(pivots, where, 1, False)
    owner = jnp.bitwise_xor(where, jnp.array(sources))
    chosen = (owner[None, :] == jnp.arange(count)[:, None])[:, :, None]
    mine = jnp.sum(jnp.where(chosen, mine[None], 0.0), axis=1)
    weights = 1.0 / mine.reshape(width_child)
    weights = jnp.concatenate([weights[:half], weights[half:][::-1]])[:, None]
    variances = pl.pallas_call(
        variance_kernel,
        grid=(STEPS,),
        in_specs=[
            pair_spec,
            pair_whole,
            row_spec,
            pl.BlockSpec((width_child, 1), lambda i: (0, 0)),
        ],
        out_specs=pl.BlockSpec((1, width_child), lambda i: (0, 0)),
        out_shape=jax.ShapeDtypeStruct((1, width_child), jnp.float32),
        compiler_params=params,
        name="variance",
    )(m, g, cross, weights)
    return root_cov, returned, variances


def solution(mesh):
    in_specs = (
        P(("groups", "row"), None),
        P(("groups", "row")),
        P(("groups", "row"), None, None),
        P("groups", "row", None),
        P("groups", "row", None, None),
        P("groups", "row"),
    )
    out_specs = (P(("groups", "row"), None), P("groups", "row", None), P(("groups", "row"), None))
    return jax.shard_map(
        on_device, mesh=mesh, in_specs=in_specs, out_specs=out_specs, check_vma=False
    )
```

```python
import jax
import jax.numpy as jnp
from jax import lax
from jax.experimental import pallas as pl
from jax.experimental.pallas import tpu as pltpu
from jax.sharding import PartitionSpec as P

BLK = 128
WIDE = 256
VMEM = 121 * 512 * 1024
VMEM_CROSS = 48 * 1024 * 1024
STEPS = 4
LIGHT = pl.CostEstimate(flops=1, bytes_accessed=1, transcendentals=0)


def split(x):
    high = x.astype(jnp.bfloat16)
    return high, (x - high.astype(jnp.float32)).astype(jnp.bfloat16)


def dot(a, b):
    return jnp.dot(a, b, preferred_element_type=jnp.float32)


def dot3(a_high, a_low, b_high, b_low):
    return dot(a_high, b_high) + (dot(a_high, b_low) + dot(a_low, b_high))


def k_range(block, half):
    start = block * WIDE
    if start < half:
        return start, 2 * half
    return half, half + 2 * half - start


def unfold(packed_ref, high_ref, low_ref):
    half, width = packed_ref.shape
    bands = half // BLK
    rows = lax.broadcasted_iota(jnp.int32, (BLK, BLK), 0)
    cols = lax.broadcasted_iota(jnp.int32, (BLK, BLK), 1)
    flip = (rows + cols == BLK - 1).astype(jnp.bfloat16)
    empty = jnp.zeros((BLK, BLK), jnp.bfloat16)
    for q in range(bands):
        here = pl.ds(q * BLK, BLK)
        there = pl.ds(half + q * BLK, BLK)
        last = 2 * bands - 1 - q
        full = packed_ref[here, : last * BLK]
        high_ref[there, : last * BLK], low_ref[there, : last * BLK] = split(full)
        mixed = packed_ref[here, last * BLK : (last + 1) * BLK]
        upper = jnp.where(
            rows + cols < BLK - 1, mixed, (rows + cols == BLK - 1).astype(jnp.float32)
        )
        edge = pl.ds(last * BLK, BLK)
        high_ref[there, edge], low_ref[there, edge] = split(upper)
        if last % 2 == 0:
            after = pl.ds((last + 1) * BLK, BLK)
            high_ref[there, after] = empty
            low_ref[there, after] = empty
        if q:
            rest = packed_ref[here, (last + 1) * BLK :]
            high_ref[here, : q * BLK], low_ref[here, : q * BLK] = split(rest)
        mixed_high, mixed_low = split(mixed)
        edge = pl.ds(q * BLK, BLK)
        diagonal = (rows == cols).astype(jnp.float32)
        high_ref[here, edge] = jnp.where(cols < rows, dot(mixed_high, flip), diagonal).astype(
            jnp.bfloat16
        )
        low_ref[here, edge] = jnp.where(cols < rows, dot(mixed_low, flip), 0.0).astype(
            jnp.bfloat16
        )
        if q % 2 == 0:
            after = pl.ds((q + 1) * BLK, BLK)
            high_ref[here, after] = empty
            low_ref[here, after] = empty


def cov_kernel(sent_ref, cov_ref, high_ref, low_ref):
    count = sent_ref.shape[0]
    width = high_ref.shape[1]
    own = high_ref.shape[0] // count
    rows = cov_ref.shape[0]

    @pl.when(pl.program_id(0) == 0)
    def _():
        for s in range(count):
            here = pl.ds(s * own, own)
            high_ref[here, :], low_ref[here, :] = split(sent_ref[s, :own, :])

    mine = pl.ds(pl.multiple_of(pl.program_id(0) * rows, rows), rows)
    left_high = high_ref[:, mine].T
    left_low = low_ref[:, mine].T
    for block in range(width // WIDE):
        cols = pl.ds(block * WIDE, WIDE)
        cov_ref[:, cols] = dot3(left_high, left_low, high_ref[:, cols], low_ref[:, cols])


def mask_kernel(pattern_ref, panel_ref, m_ref):
    height, width = panel_ref.shape
    blocks = width // BLK
    rows = lax.broadcasted_iota(jnp.int32, (BLK, BLK), 0)
    cols = lax.broadcasted_iota(jnp.int32, (BLK, BLK), 1)
    flip = (rows + cols == BLK - 1).astype(jnp.bfloat16)
    for b in range(blocks):
        block = panel_ref[:, b * BLK : (b + 1) * BLK]
        here = pattern_ref[pl.program_id(0), b].astype(jnp.float32)
        high, low = split(block * here)
        place = b
        if b >= blocks // 2:
            high = dot(high, flip).astype(jnp.bfloat16)
            low = dot(low, flip).astype(jnp.bfloat16)
            place = blocks // 2 + blocks - 1 - b
        to = pl.ds(place * BLK, BLK)
        m_ref[0, :, to] = high
        m_ref[1, :, to] = low


def turn_kernel(cov_ref, m_ref, t_ref):
    cov_high, cov_low = split(cov_ref[...])
    for block in range(m_ref.shape[2] // WIDE):
        cols = pl.ds(block * WIDE, WIDE)
        t_ref[0, :, cols], t_ref[1, :, cols] = split(
            -dot3(cov_high, cov_low, m_ref[0, :, cols], m_ref[1, :, cols])
        )


def cross_kernel(t_ref, packed_ref, out_ref, g_ref, t, g, out, came, left, kept):
    half, width = packed_ref.shape
    rows = out.shape[0] // STEPS
    arriving, leaving = [], []
    for step in range(STEPS):
        here = pl.ds(step * rows, rows)
        arriving.append(pltpu.make_async_copy(t_ref.at[:, here], t.at[:, here], came.at[step]))
        leaving.append(pltpu.make_async_copy(out.at[here], out_ref.at[here], left.at[step]))
    keeping = pltpu.make_async_copy(g, g_ref, kept)
    for copy in arriving:
        copy.start()
    unfold(packed_ref, g.at[0], g.at[1])
    keeping.start()
    for step in range(STEPS):
        here = pl.ds(step * rows, rows)
        arriving[step].wait()
        for block in range(width // WIDE):
            first, stop = k_range(block, half)
            cols = pl.ds(block * WIDE, WIDE)
            out[here, cols] = dot3(
                t[0, here, first:stop],
                t[1, here, first:stop],
                g[0, first:stop, cols],
                g[1, first:stop, cols],
            )
        leaving[step].start()
    for copy in leaving:
        copy.wait()
    keeping.wait()


def copy_kernel(from_ref, to_ref, held, came, left):
    parts = came.shape[0]
    each = held.shape[0] // parts
    pieces = [pl.ds(part * each, each) for part in range(parts)]
    arriving = [
        pltpu.make_async_copy(from_ref.at[here], held.at[here], came.at[part])
        for part, here in enumerate(pieces)
    ]
    leaving = [
        pltpu.make_async_copy(held.at[here], to_ref.at[here], left.at[part])
        for part, here in enumerate(pieces)
    ]
    for copy in arriving:
        copy.start()
    for came_in, leave in zip(arriving, leaving):
        came_in.wait()
        leave.start()
    for copy in leaving:
        copy.wait()


def variance_kernel(m_ref, g_ref, cross_ref, weight_ref, out_ref):
    _, height, width = g_ref.shape

    @pl.when(pl.program_id(0) == 0)
    def _():
        for block in range(width // WIDE):
            first, stop = k_range(block, height // 2)
            cols = pl.ds(block * WIDE, WIDE)
            entries = g_ref[0, first:stop, cols].astype(jnp.float32)
            entries += g_ref[1, first:stop, cols].astype(jnp.float32)
            out_ref[:, cols] = jnp.sum(
                entries * entries * weight_ref[first:stop, :], axis=0, keepdims=True
            )

    for block in range(width // WIDE):
        first, stop = k_range(block, height // 2)
        cols = pl.ds(block * WIDE, WIDE)
        scaled = dot3(
            m_ref[0, :, first:stop],
            m_ref[1, :, first:stop],
            g_ref[0, first:stop, cols],
            g_ref[1, first:stop, cols],
        )
        out_ref[:, cols] -= jnp.sum(scaled * cross_ref[:, cols], axis=0, keepdims=True)


def pack(child_inverse, where):
    children, fold, _, width = child_inverse.shape
    blocks = width // BLK
    low = child_inverse[:, :, 0, :]
    high = child_inverse[:, :, 1, :]
    q = (where * fold) // BLK
    rows = (where * fold) % BLK + jnp.arange(fold)[:, None]
    spot = jnp.arange(BLK)[None, :]
    low_edge = lax.dynamic_slice_in_dim(low, q * BLK, BLK, 2)[:, :, ::-1]
    moved = lax.dynamic_slice_in_dim(
        jnp.concatenate([low, low], axis=2), q * BLK, width, 2
    )
    high_edge = lax.dynamic_slice_in_dim(high, (blocks - 1 - q) * BLK, BLK, 2)
    edge = jnp.where(spot + rows < BLK - 1, high_edge, low_edge)
    block = jnp.arange(width) // BLK
    packed = jnp.where(block < blocks - 1 - q, high, moved)
    return lax.dynamic_update_slice_in_dim(packed, edge, (blocks - 1 - q) * BLK, 2)


def swap(x, count, bit):
    return lax.ppermute(x, "row", [(i, i ^ bit) for i in range(count)])


def scale(inverse, pivots):
    rows, width = inverse.shape
    child_pivots = pivots[0, :-rows].reshape(-1, width)
    child_pivots = jnp.pad(child_pivots, ((0, -child_pivots.shape[0] % 8), (0, 0)))
    return inverse * lax.rsqrt(pivots[0, -rows:])[:, None], child_pivots


def spread(held, sources, count, bit):
    held = jnp.concatenate([held, swap(held, count, bit)])
    return held, sources + [s ^ bit for s in sources]


def exchange(x):
    return lax.all_to_all(x, "row", split_axis=0, concat_axis=0, tiled=True)


def on_device(root_inverse, root_pivots, pattern, cross_factor, child_inverse, child_pivots):
    count = lax.axis_size("row")
    where = lax.axis_index("row")
    own_rows, width_root = root_inverse.shape
    children, _, width_child = cross_factor.shape
    assert children == count
    half = width_child // 2

    packed = pack(child_inverse, where)

    bits = [count // 2, *(1 << k for k in range(1, count.bit_length() - 2)), 1]
    pivots = jnp.concatenate([child_pivots.reshape(-1), root_pivots])[None]
    far_inverse, far_pivots, panels = lax.optimization_barrier(
        (swap(root_inverse, count, bits[0]), swap(pivots, count, bits[0]), cross_factor)
    )
    sent = [*scale(root_inverse, pivots), *scale(far_inverse, far_pivots)]
    sent, sources = jnp.concatenate(sent), [0, bits[0]]
    panels = exchange(panels)
    for bit in bits[1:]:
        sent, sources = spread(sent, sources, count, bit)
    packed = exchange(packed).reshape(half, width_child)

    sent = sent.reshape(count, -1, width_root)
    pivots = sent[:, own_rows:].reshape(count, -1)
    pivots = pivots[:, : children * own_rows].reshape(count, children, own_rows)

    rows = width_root // STEPS
    row_spec = pl.BlockSpec((rows, width_child), lambda i: (i, 0))
    pair_spec = pl.BlockSpec((2, rows, width_child), lambda i: (0, i, 0))
    band = pl.BlockSpec((BLK, width_child), lambda i: (i, 0))
    pair = jax.ShapeDtypeStruct((2, width_root, width_child), jnp.bfloat16)
    pair_whole = pl.BlockSpec((2, width_root, width_child), lambda i: (0, 0, 0))
    anywhere = pl.BlockSpec(memory_space=pltpu.HBM)
    params = pltpu.CompilerParams(vmem_limit_bytes=VMEM)
    whole_cov = pl.pallas_call(
        cov_kernel,
        grid=(STEPS,),
        in_specs=[pl.BlockSpec(sent.shape, lambda i: (0, 0, 0))],
        out_specs=pl.BlockSpec((rows, width_root), lambda i: (i, 0)),
        out_shape=jax.ShapeDtypeStruct((width_root, width_root), jnp.float32),
        scratch_shapes=[pltpu.VMEM((width_root, width_root), jnp.bfloat16)] * 2,
        compiler_params=params,
        cost_estimate=pl.CostEstimate(flops=6 * width_root**3, bytes_accessed=16 << 20, transcendentals=0),
        name="cov",
    )(sent)
    root_cov = lax.dynamic_slice_in_dim(whole_cov, where * own_rows, own_rows, 0)

    m = pl.pallas_call(
        mask_kernel,
        grid=(width_root // BLK,),
        in_specs=[pl.BlockSpec(memory_space=pltpu.SMEM), band],
        out_specs=pl.BlockSpec((2, BLK, width_child), lambda i: (0, i, 0)),
        out_shape=pair,
        compiler_params=params,
        cost_estimate=LIGHT,
        name="mask",
    )(pattern[0], panels.reshape(width_root, width_child))
    t = pl.pallas_call(
        turn_kernel,
        grid=(STEPS,),
        in_specs=[pl.BlockSpec((rows, width_root), lambda i: (i, 0)), pair_whole],
        out_specs=pair_spec,
        out_shape=pair,
        compiler_params=params,
        cost_estimate=LIGHT,
        name="turn",
    )(whole_cov, m)
    cross, g = pl.pallas_call(
        cross_kernel,
        in_specs=[anywhere, pl.BlockSpec(memory_space=pltpu.VMEM)],
        out_specs=[anywhere, anywhere],
        out_shape=[
            jax.ShapeDtypeStruct((width_root, width_child), jnp.float32),
            jax.ShapeDtypeStruct((2, width_child, width_child), jnp.bfloat16),
        ],
        scratch_shapes=[
            pltpu.VMEM((2, width_root, width_child), jnp.bfloat16),
            pltpu.VMEM((2, width_child, width_child), jnp.bfloat16),
            pltpu.VMEM((width_root, width_child), jnp.float32),
            pltpu.SemaphoreType.DMA((STEPS,)),
            pltpu.SemaphoreType.DMA((STEPS,)),
            pltpu.SemaphoreType.DMA(()),
        ],
        compiler_params=pltpu.CompilerParams(vmem_limit_bytes=VMEM_CROSS),
        name="cross",
    )(t, packed)

    returned = exchange(cross.reshape(children, own_rows, width_child))
    returned = pl.pallas_call(
        copy_kernel,
        in_specs=[anywhere],
        out_specs=anywhere,
        out_shape=jax.ShapeDtypeStruct(returned.shape, returned.dtype),
        scratch_shapes=[
            pltpu.VMEM(returned.shape, returned.dtype),
            pltpu.SemaphoreType.DMA((8,)),
            pltpu.SemaphoreType.DMA((8,)),
        ],
        compiler_params=params,
        name="place",
    )(returned)

    mine = lax.dynamic_index_in_dim(pivots, where, 1, False)
    owner = jnp.bitwise_xor(where, jnp.array(sources))
    chosen = (owner[None, :] == jnp.arange(count)[:, None])[:, :, None]
    mine = jnp.sum(jnp.where(chosen, mine[None], 0.0), axis=1)
    weights = 1.0 / mine.reshape(width_child)
    weights = jnp.concatenate([weights[:half], weights[half:][::-1]])[:, None]
    variances = pl.pallas_call(
        variance_kernel,
        grid=(STEPS,),
        in_specs=[
            pair_spec,
            pair_whole,
            row_spec,
            pl.BlockSpec((width_child, 1), lambda i: (0, 0)),
        ],
        out_specs=pl.BlockSpec((1, width_child), lambda i: (0, 0)),
        out_shape=jax.ShapeDtypeStruct((1, width_child), jnp.float32),
        compiler_params=params,
        name="variance",
    )(m, g, cross, weights)
    return root_cov, returned, variances


def solution(mesh):
    in_specs = (
        P(("groups", "row"), None),
        P(("groups", "row")),
        P(("groups", "row"), None, None),
        P("groups", "row", None),
        P("groups", "row", None, None),
        P("groups", "row"),
    )
    out_specs = (P(("groups", "row"), None), P("groups", "row", None), P(("groups", "row"), None))
    return jax.shard_map(
        on_device, mesh=mesh, in_specs=in_specs, out_specs=out_specs, check_vma=False
    )
```
